32 devices in a mesh: tok: 8 (over z, x), exp: 4 (over y, core).
Axes of the slice: x: 2, y: 2, z: 4, core: 2. Of those that a mesh axis runs over, the one named last changes fastest.
Arguments:
- tokens_x: bfloat16 [1280, 4096], P('tok', 'exp'), may hold values from -6 to 6
- out_grad: bfloat16 [1280, 4096], P('tok', 'exp'), may hold values from -12 to 12
- expert_ids: int32 [1280, 8], P('tok'), may hold values from 0 to 31, as said below
- route_q: int32 [1280, 8], P('tok'), may hold values from 1 to 255
- gate_w: bfloat16 [4, 1536, 4096], P('exp', 'tok'), may hold values from -0.09375 to 0.09375
- up_w: bfloat16 [4, 1536, 4096], P('exp', 'tok'), may hold values from -0.09375 to 0.09375
- down_w: bfloat16 [4, 1536, 4096], P('exp', 'tok'), may hold values from -0.15625 to 0.15625
Outputs:
- input_factor: float32 [4, 4096, 4096], P('exp', 'tok')
- grad_factor: float32 [4, 1536, 1536], P('exp', 'tok')
The draws below stay inside these ranges and needn't reach their ends.
Inputs may be any that keep to these rules, and one draw needn't show every extreme that they name: `expert_ids`: each token names exactly one expert from each range of 4 ids that starts at a multiple of 4, in varying positions of its row. Within the rows of one index of tok (aligned blocks of 160 rows) no expert below 4 is named by more than 80 rows, and in every draw one expert below 4 is named by exactly 80 rows in every block.
All inputs are finite; a program needn't handle non-finite values.
Results may differ from the reference program's by a relative error of at most 0.0056.
Values may be sent and summed in bfloat16 or wider, within the bound.
A program may use at most 64 MiB of HBM per device.

```python
import jax
import jax.numpy as jnp
from jax import lax

D = 4096
FF = 1536
TOPK = 8
TOK_DEV = 160
TOKENS = 1280
CAP = 80
ROWS = 640
N_TOK = 8
N_EXP = 4


def rank_block(block_key):
    return jax.random.permutation(block_key, TOK_DEV)


def other_block(block_key):
    return jax.random.permutation(block_key, N_EXP - 1)


def draw_expert_ids(key, part):
    key_star, key_rank, key_other, key_rest, key_turn = jax.random.split(key, 5)
    blocks = TOKENS // TOK_DEV
    favored = jax.random.randint(key_star, (), 0, N_EXP)
    ranking = jax.vmap(rank_block)(jax.random.split(key_rank, blocks))
    others = jax.vmap(other_block)(jax.random.split(key_other, blocks))
    spill = jnp.maximum(ranking - CAP, 0) % (N_EXP - 1)
    other_ids = (favored + 1 + jnp.take_along_axis(others, spill, axis=1)) % N_EXP
    chosen = jnp.where(ranking < CAP, favored, other_ids).reshape(TOKENS)
    remaining = jax.random.randint(key_rest, (TOKENS, TOPK - 1), 0, N_EXP)
    offsets = jnp.arange(1, TOPK, dtype=jnp.int32) * N_EXP
    listed = jnp.concatenate([chosen[:, None], remaining + offsets[None, :]], axis=1)
    rotation = jax.random.randint(key_turn, (TOKENS, 1), 0, TOPK)
    ordering = (jnp.arange(TOPK, dtype=jnp.int32)[None, :] + rotation) % TOPK
    return jnp.take_along_axis(listed, ordering, axis=1).astype(jnp.int32)


def set_ends(entries, stream_key, low, top_value):
    longest = entries.shape.index(max(entries.shape))
    spots = []
    for shift in (0, 1):
        where = [jax.random.randint(jax.random.fold_in(stream_key, axis), (), 0, length) for axis, length in enumerate(entries.shape)]
        where[longest] = (where[longest] + shift) % entries.shape[longest]
        spots.append(tuple(where))
    return entries.at[spots[0]].set(low).at[spots[1]].set(top_value)


def shard_levels(own_key, shape, cuts, least, largest):
    factor_of = 1.0
    for axis_at, blocks in cuts:
        steps = jax.random.uniform(jax.random.fold_in(jax.random.fold_in(own_key, 6), axis_at), (blocks,), jnp.float32, least / len(cuts), largest / len(cuts))
        factor_of = factor_of * jnp.repeat(jnp.exp(steps), shape[axis_at] // blocks).reshape((-1,) + (1,) * (len(shape) - 1 - axis_at))
    return factor_of


def bell_draw(own_key, extent, spread, reach, shards=(), kind=jnp.bfloat16):
    array = spread * jax.random.normal(own_key, extent, jnp.float32)
    if shards:
        array = array * shard_levels(own_key, extent, shards, -0.22, 0.18)
    return jnp.clip(array, -reach, reach).astype(kind)


def setup_inputs(seed: int = 0) -> dict:
    splits = jax.random.split(jax.random.key(seed), 8)
    return {
        "tokens_x": bell_draw(splits[0], (TOKENS, D), 1.0, 6.0, ((0, 8), (1, 4))),
        "out_grad": bell_draw(splits[1], (TOKENS, D), 3.0, 12.0, ((0, 8), (1, 4))),
        "expert_ids": draw_expert_ids(jax.random.fold_in(splits[7], 71), 0),
        "route_q": set_ends(jax.random.randint(splits[3], (TOKENS, TOPK), 1, 256), jax.random.fold_in(splits[3], 1), 1, 255).astype(jnp.int32),
        "gate_w": bell_draw(splits[4], (N_EXP, FF, D), D ** -0.5, 0.09375, ((0, 4), (1, 8))),
        "up_w": bell_draw(splits[5], (N_EXP, FF, D), D ** -0.5, 0.09375, ((0, 4), (1, 8))),
        "down_w": bell_draw(splits[6], (N_EXP, FF, D), FF ** -0.5, 0.15625, ((0, 4), (1, 8))),
    }


def silu_slope(values):
    sigma = jax.nn.sigmoid(values)
    return sigma * (1.0 + values * (1.0 - sigma))


def reference(tokens_x, out_grad, expert_ids, route_q, gate_w, up_w, down_w):
    fitted = expert_ids < N_EXP
    fitted_id = jnp.sum(jnp.where(fitted, expert_ids, 0), axis=1).astype(jnp.int32)
    route_weight = jnp.sum(jnp.where(fitted, route_q, 0), axis=1).astype(jnp.float32) / 256.0
    onehot = (fitted_id[:, None] == jnp.arange(N_EXP, dtype=jnp.int32)[None, :]).astype(jnp.int32)
    running = jnp.cumsum(onehot.reshape(N_TOK, TOK_DEV, N_EXP), axis=1).astype(jnp.int32)
    running = running.reshape(TOKENS, N_EXP)
    rank_in = (jnp.sum(running * onehot, axis=1) - 1).astype(jnp.int32)
    shard_of = (jnp.arange(TOKENS, dtype=jnp.int32) // TOK_DEV).astype(jnp.int32)
    slot_ids = (fitted_id * ROWS + shard_of * CAP + rank_in).astype(jnp.int32)
    scaled_grad = (route_weight[:, None] * out_grad.astype(jnp.float32)).astype(jnp.bfloat16)
    x_slots = jnp.zeros((N_EXP * ROWS, D), jnp.bfloat16).at[slot_ids].set(tokens_x)
    g_slots = jnp.zeros((N_EXP * ROWS, D), jnp.bfloat16).at[slot_ids].set(scaled_grad)
    x_slots = x_slots.reshape(N_EXP, ROWS, D)
    g_slots = g_slots.reshape(N_EXP, ROWS, D)

    def per_expert(operand):
        x_rows, g_rows, w_gate, w_up, w_down = operand
        gate_pre = jnp.dot(x_rows, w_gate.T, preferred_element_type=jnp.float32)
        up_pre = jnp.dot(x_rows, w_up.T, preferred_element_type=jnp.float32)
        hidden_grad = jnp.dot(g_rows, w_down.T, preferred_element_type=jnp.float32)
        gate_grad = (hidden_grad * up_pre * silu_slope(gate_pre)).astype(jnp.bfloat16)
        in_factor = jnp.dot(x_rows.T, x_rows, preferred_element_type=jnp.float32) / ROWS
        grad_out = jnp.dot(gate_grad.T, gate_grad, preferred_element_type=jnp.float32) / ROWS
        return in_factor, grad_out

    input_factor, grad_factor = lax.map(per_expert, (x_slots, g_slots, gate_w, up_w, down_w))
    return (input_factor, grad_factor)
```

```python
import functools

import jax
import jax.numpy as jnp
from jax import lax
from jax.experimental import pallas as pl
from jax.experimental.pallas import tpu as pltpu
from jax.sharding import PartitionSpec as P

MESH = pl.DeviceIdType.MESH
NT = (((1,), (1,)), ((), ()))


def silu_slope(values):
    sigma = jax.nn.sigmoid(values)
    return sigma * (1.0 + values * (1.0 - sigma))


def ring_place(index, count):
    odd = lax.rem(index, 2)
    half = index // 2
    return (1 - odd) * half + odd * (count - 1 - half)


def ring_index(place, count):
    place = lax.rem(place + 2 * count, count)
    late = place // (count // 2)
    return (1 - late) * (2 * place) + late * (2 * (count - 1 - place) + 1)


def exchange_kernel(
    shards, owners,
    px_ref, pg_ref, wg_ref, wu_ref, wd_ref,
    x_out, gg_out,
    xbuf, gbuf, wg, wu, wd, acc, factor, gg,
    swap_send, swap_recv, own_sem, ring_send, ring_recv, gg_send, gg_recv, load_sem, store_sem,
):
    tok = lax.axis_index("tok")
    exp = lax.axis_index("exp")
    place = ring_place(tok, shards)
    ahead = ring_index(place + 1, shards)
    behind = ring_index(place - 1, shards)
    width = px_ref.shape[2]
    full = xbuf.shape[2]
    cap = xbuf.shape[1]
    far = shards // 2
    near = (shards - 1) // 2

    barrier = pltpu.get_barrier_semaphore()
    for neighbour in (ahead, behind):
        pl.semaphore_signal(barrier, inc=1, device_id=(neighbour, exp), device_id_type=MESH)
    for k in range(1, owners):
        pl.semaphore_signal(
            barrier, inc=1, device_id=(tok, lax.rem(exp + k, owners)), device_id_type=MESH
        )
    pl.semaphore_wait(barrier, owners + 1)

    sent = []
    columns = pl.ds(pl.multiple_of(exp * width, 128), width)
    swaps = [[], []]
    for a, (packed, buf) in enumerate(((px_ref, xbuf), (pg_ref, gbuf))):
        for k in range(1, owners):
            peer = lax.rem(exp + k, owners)
            copy = pltpu.make_async_remote_copy(
                src_ref=packed.at[peer],
                dst_ref=buf.at[tok, :, columns],
                send_sem=swap_send.at[a, k],
                recv_sem=swap_recv.at[a, k],
                device_id=(tok, peer),
                device_id_type=MESH,
            )
            copy.start()
            sent.append(copy)
            swaps[a].append(copy)
        own = pltpu.make_async_copy(packed.at[exp], buf.at[tok, :, columns], own_sem.at[a])
        own.start()
        swaps[a].append(own)

    loads = []
    for i, (src, dst) in enumerate(((wg_ref, wg), (wu_ref, wu), (wd_ref, wd))):
        load = pltpu.make_async_copy(src, dst, load_sem.at[i])
        load.start()
        loads.append(load)

    def finish_swap(a):
        for copy in swaps[a][:-1]:
            copy.wait_recv()
        swaps[a][-1].wait()

    half = full // 2
    bufs = (xbuf, gbuf)
    copies = {}

    def send(a, d, hop, c):
        block = ring_index(place - hop if d == 0 else place + hop, shards)
        view = bufs[a].at[block, :, pl.ds(c * half, half)]
        copy = pltpu.make_async_remote_copy(
            src_ref=view,
            dst_ref=view,
            send_sem=ring_send.at[a, d, hop, c],
            recv_sem=ring_recv.at[a, d, hop, c],
            device_id=(ahead if d == 0 else behind, exp),
            device_id_type=MESH,
        )
        copy.start()
        sent.append(copy)
        copies[a, d, hop, c] = copy

    def product(weights, buf):
        rows = buf.shape[0] * cap
        step = min(1024, full)
        acc[...] = jnp.zeros_like(acc)

        def body(i, carry):
            part = pl.ds(pl.multiple_of(i * step, step), step)
            acc[...] += lax.dot_general(
                weights[:, part],
                buf[:, :, part].reshape(rows, step),
                NT,
                preferred_element_type=jnp.float32,
            )
            return carry

        lax.fori_loop(0, full // step, body, 0)

    orders = (
        [(0, h) for h in range(far)] + [(1, h) for h in range(near)],
        [(0, h) for h in range(near)] + [(1, h) for h in range(far)],
    )
    swapped = set()
    store_x = pltpu.make_async_copy(xbuf, x_out, store_sem.at[0])
    for s in range(far + near):
        for c in range(2):
            for d in range(2):
                a, hop = orders[d][s]
                if hop == 0:
                    if a not in swapped:
                        finish_swap(a)
                        swapped.add(a)
                else:
                    copies[a, d, hop - 1, c].wait_recv()
                send(a, d, hop, c)
        if s == far:
            for c in range(2):
                copies[0, 0, far - 1, c].wait_recv()
                copies[0, 1, near - 1, c].wait_recv()
            store_x.start()
            loads[0].wait()
            product(wg, xbuf)
            factor[...] = silu_slope(acc[...])
        if s == far + 1:
            loads[1].wait()
            product(wu, xbuf)
            factor[...] = factor[...] * acc[...]

    for c in range(2):
        copies[1, 0, near - 1, c].wait_recv()
        copies[1, 1, far - 1, c].wait_recv()
    loads[2].wait()
    product(wd, gbuf)
    gg[tok] = (acc[...] * factor[...]).astype(gg.dtype)

    units = gg.shape[1]
    first = -(-(units // 2) // 16) * 16
    cuts = (pl.ds(0, first), pl.ds(first, units - first))
    gg_copies = {}
    for hop in range(far):
        for c in range(2):
            for d in range(2):
                if hop >= near and c != d:
                    continue
                if hop > 0:
                    gg_copies[d, hop - 1, c].wait_recv()
                block = ring_index(place - hop if d == 0 else place + hop, shards)
                view = gg.at[block, cuts[c], :]
                copy = pltpu.make_async_remote_copy(
                    src_ref=view,
                    dst_ref=view,
                    send_sem=gg_send.at[d, hop, c],
                    recv_sem=gg_recv.at[d, hop, c],
                    device_id=(ahead if d == 0 else behind, exp),
                    device_id_type=MESH,
                )
                copy.start()
                sent.append(copy)
                gg_copies[d, hop, c] = copy
    for (d, hop, c), copy in gg_copies.items():
        if (d, hop + 1, c) not in gg_copies:
            copy.wait_recv()
    store_gg = pltpu.make_async_copy(gg, gg_out, store_sem.at[1])
    store_gg.start()
    for copy in sent:
        copy.wait_send()
    store_x.wait()
    store_gg.wait()


def local(tokens_x, out_grad, expert_ids, route_q, gate_w, up_w, down_w):
    owners = lax.axis_size("exp")
    shards = lax.axis_size("tok")
    position = lax.axis_index("tok")
    tok_rows = tokens_x.shape[0]
    local_width = tokens_x.shape[1]
    capacity = 2 * tok_rows // owners
    slot_count = capacity * shards
    padded = -(-capacity // 16) * 16
    fitted = expert_ids < owners
    fitted_id = jnp.sum(jnp.where(fitted, expert_ids, 0), axis=1)
    route_weight = jnp.sum(jnp.where(fitted, route_q, 0), axis=1).astype(jnp.float32) / 256.0
    order = jnp.arange(tok_rows, dtype=jnp.int32)
    earlier = (fitted_id[:, None] == fitted_id[None, :]) & (order[:, None] > order[None, :])
    rank_in = jnp.sum(earlier.astype(jnp.int32), axis=1)
    slot_ids = fitted_id * padded + rank_in
    packer = (slot_ids[None, :] == jnp.arange(owners * padded, dtype=jnp.int32)[:, None]).astype(
        jnp.bfloat16
    )
    scaled = (route_weight[:, None] * out_grad.astype(jnp.float32)).astype(jnp.bfloat16)
    packed_x = jnp.dot(packer, tokens_x, preferred_element_type=jnp.float32).astype(jnp.bfloat16)
    packed_g = jnp.dot(packer, scaled, preferred_element_type=jnp.float32).astype(jnp.bfloat16)
    packed_x = packed_x.reshape(owners, padded, local_width)
    packed_g = packed_g.reshape(owners, padded, local_width)
    full_width = local_width * owners
    units = gate_w.shape[1]
    rows = shards * padded
    far = shards // 2
    vmem = pl.BlockSpec(memory_space=pltpu.VMEM)
    anywhere = pl.BlockSpec(memory_space=pl.ANY)
    dma = pltpu.SemaphoreType.DMA
    x_all, gg_all = pl.pallas_call(
        functools.partial(exchange_kernel, shards, owners),
        out_shape=(
            jax.ShapeDtypeStruct((shards, padded, full_width), jnp.bfloat16),
            jax.ShapeDtypeStruct((shards, units, rows), jnp.bfloat16),
        ),
        in_specs=[vmem, vmem, anywhere, anywhere, anywhere],
        out_specs=(anywhere, anywhere),
        scratch_shapes=[
            pltpu.VMEM((shards, padded, full_width), jnp.bfloat16),
            pltpu.VMEM((shards, padded, full_width), jnp.bfloat16),
            pltpu.VMEM((units, full_width), jnp.bfloat16),
            pltpu.VMEM((units, full_width), jnp.bfloat16),
            pltpu.VMEM((units, full_width), jnp.bfloat16),
            pltpu.VMEM((units, rows), jnp.float32),
            pltpu.VMEM((units, rows), jnp.float32),
            pltpu.VMEM((shards, units, rows), jnp.bfloat16),
            dma((2, owners)),
            dma((2, owners)),
            dma((2,)),
            dma((2, 2, far, 2)),
            dma((2, 2, far, 2)),
            dma((2, far, 2)),
            dma((2, far, 2)),
            dma((3,)),
            dma((2,)),
        ],
        compiler_params=pltpu.CompilerParams(
            collective_id=0, has_side_effects=True, vmem_limit_bytes=48 * 2**20
        ),
        cost_estimate=pl.CostEstimate(
            flops=6 * units * rows * full_width,
            bytes_accessed=20 * 2**20,
            transcendentals=units * rows,
        ),
    )(packed_x, packed_g, gate_w[0], up_w[0], down_w[0])
    all_rows = x_all.reshape(rows, full_width)
    strip_width = full_width // shards
    column_strip = lax.dynamic_slice_in_dim(all_rows, position * strip_width, strip_width, 1)
    input_rows = lax.dot_general(
        column_strip, all_rows, (((0,), (0,)), ((), ())), preferred_element_type=jnp.float32
    )
    input_rows = input_rows / float(slot_count)
    grad_cols = lax.dynamic_index_in_dim(gg_all, position, 0, keepdims=False)
    grad_rows = lax.dot_general(
        grad_cols, gg_all.reshape(shards * units, rows), NT, preferred_element_type=jnp.float32
    )
    grad_rows = grad_rows / float(slot_count)
    return (input_rows[None], grad_rows[None])


def solution(mesh):
    placed = (
        P("tok", "exp"),
        P("tok", "exp"),
        P("tok", None),
        P("tok", None),
        P("exp", "tok", None),
        P("exp", "tok", None),
        P("exp", "tok", None),
    )
    return jax.shard_map(
        local,
        mesh=mesh,
        in_specs=placed,
        out_specs=(P("exp", "tok", None), P("exp", "tok", None)),
        check_vma=False,
    )
```

```python
import functools

import jax
import jax.numpy as jnp
from jax import lax
from jax.experimental import pallas as pl
from jax.experimental.pallas import tpu as pltpu
from jax.sharding import PartitionSpec as P

MESH = pl.DeviceIdType.MESH
NT = (((1,), (1,)), ((), ()))


def silu_slope(values):
    sigma = jax.nn.sigmoid(values)
    return sigma * (1.0 + values * (1.0 - sigma))


def ring_place(index, count):
    odd = lax.rem(index, 2)
    half = index // 2
    return (1 - odd) * half + odd * (count - 1 - half)


def ring_index(place, count):
    place = lax.rem(place + 2 * count, count)
    late = place // (count // 2)
    return (1 - late) * (2 * place) + late * (2 * (count - 1 - place) + 1)


def exchange_kernel(
    shards, owners, slot_count,
    px_ref, raw_ref, ids_ref, wg_ref, wu_ref, wd_ref,
    in_out, gg_out,
    xbuf, gbuf, raw, packed, ids, wg, wu, wd, acc, factor, gg, strip, wide,
    ids_send, ids_recv, swap_send, swap_recv, own_sem, ring_send, ring_recv,
    gg_send, gg_recv, load_sem, store_sem,
):
    tok = lax.axis_index("tok")
    exp = lax.axis_index("exp")
    place = ring_place(tok, shards)
    ahead = ring_index(place + 1, shards)
    behind = ring_index(place - 1, shards)
    width = px_ref.shape[2]
    full = xbuf.shape[2]
    cap = xbuf.shape[1]
    rows = shards * cap
    far = shards // 2
    near = (shards - 1) // 2

    barrier = pltpu.get_barrier_semaphore()
    for k in range(1, shards):
        pl.semaphore_signal(
            barrier, inc=1, device_id=(lax.rem(tok + k, shards), exp), device_id_type=MESH
        )
    for k in range(1, owners):
        pl.semaphore_signal(
            barrier, inc=1, device_id=(tok, lax.rem(exp + k, owners)), device_id_type=MESH
        )
    pl.semaphore_wait(barrier, shards + owners - 2)

    sent = []

    def remote(src, dst, send_sem, recv_sem, device):
        copy = pltpu.make_async_remote_copy(
            src_ref=src,
            dst_ref=dst,
            send_sem=send_sem,
            recv_sem=recv_sem,
            device_id=device,
            device_id_type=MESH,
        )
        copy.start()
        sent.append(copy)
        return copy

    copies = {}

    def send(a, d, hop, c):
        block = ring_index(place - hop if d == 0 else place + hop, shards)
        buf = (raw, xbuf)[a]
        half = buf.shape[2] // 2
        view = buf.at[block, :, pl.ds(c * half, half)]
        src = raw_ref.at[:, pl.ds(c * half, half)] if a == 0 and hop == 0 else view
        copies[a, d, hop, c] = remote(
            src,
            view,
            ring_send.at[a, d, hop, c],
            ring_recv.at[a, d, hop, c],
            (ahead if d == 0 else behind, exp),
        )

    columns = pl.ds(pl.multiple_of(exp * width, 128), width)
    swaps = []

    def swap(j, source, buf, block):
        for k in range(1, owners):
            peer = lax.rem(exp + k, owners)
            swaps.append((j, remote(
                source(peer),
                buf.at[block, :, columns],
                swap_send.at[j, k],
                swap_recv.at[j, k],
                (tok, peer),
            ).wait_recv))
        own = pltpu.make_async_copy(source(exp), buf.at[block, :, columns], own_sem.at[j])
        own.start()
        swaps.append((j, own.wait))

    slot_iota = lax.broadcasted_iota(jnp.int32, (owners * cap, ids.shape[2]), 0)

    def pack(j, block, tokens):
        picks = (slot_iota == ids[block, 0:1, :]).astype(jnp.float32).astype(jnp.bfloat16)
        chosen = jnp.dot(picks, tokens, preferred_element_type=jnp.float32)
        packed[block] = chosen.astype(jnp.bfloat16).reshape(owners, cap, width)
        swap(j, lambda e: packed.at[block, e], gbuf, block)

    id_copies = []

    orders = (
        [(0, h) for h in range(far)] + [(1, h) for h in range(near)],
        [(0, h) for h in range(near)] + [(1, h) for h in range(far)],
    )
    for c in range(2):
        for d in range(2):
            send(0, d, 0, c)
    ids[tok] = ids_ref[...]
    for k in range(1, shards):
        id_copies.append(remote(
            ids_ref, ids.at[tok], ids_send.at[k], ids_recv.at[k], (lax.rem(tok + k, shards), exp)
        ))
    swap(0, lambda e: px_ref.at[e], xbuf, tok)
    pack(1, tok, raw_ref[...])
    number = 2

    loads = []
    for i, (src, dst) in enumerate(((wd_ref, wd), (wg_ref, wg), (wu_ref, wu))):
        load = pltpu.make_async_copy(src, dst, load_sem.at[i])
        load.start()
        loads.append(load)

    for copy in id_copies:
        copy.wait_recv()

    x_ready = False
    for s in range(1, far + near):
        landed = []
        for c in range(2):
            for d in range(2):
                a, hop = orders[d][s - 1]
                copies[a, d, hop, c].wait_recv()
                if c == 1 and a == 0:
                    landed.append((d, hop + 1))
                if orders[d][s] == (1, 0) and not x_ready:
                    for j, wait in swaps:
                        if j == 0:
                            wait()
                    x_ready = True
                send(*(orders[d][s][0], d, orders[d][s][1], c))
        for d, hop in landed:
            block = ring_index(place - hop if d == 0 else place + hop, shards)
            pack(number, block, raw[block])
            number += 1

    def product(weights, buf):
        step = min(1024, full)
        acc[...] = jnp.zeros_like(acc)

        def body(i, carry):
            part = pl.ds(pl.multiple_of(i * step, step), step)
            acc[...] += lax.dot_general(
                weights[:, part],
                buf[:, :, part].reshape(rows, step),
                NT,
                preferred_element_type=jnp.float32,
            )
            return carry

        lax.fori_loop(0, full // step, body, 0)

    for j, wait in swaps:
        if j > 0:
            wait()
    for load in loads:
        load.wait()
    product(wd, gbuf)
    factor[...] = acc[...]
    for c in range(2):
        for d in range(2):
            copies[1, d, orders[d][-1][1], c].wait_recv()
    product(wu, xbuf)
    factor[...] = factor[...] * acc[...]
    product(wg, xbuf)
    gg[tok] = (factor[...] * silu_slope(acc[...])).astype(gg.dtype)

    tile = min(512, full)
    tiles = full // tile
    strip_width = strip.shape[0]

    def input_tiles(low, high):
        def body(i, carry):
            part = pl.ds(pl.multiple_of(i * tile, tile), tile)
            total = jnp.dot(
                strip[...], xbuf[:, :, part].reshape(rows, tile), preferred_element_type=jnp.float32
            )
            wide[:, part] = total / float(slot_count)
            return carry

        lax.fori_loop(low, high, body, 0)

    units = gg.shape[1]
    first = -(-(units // 2) // 16) * 16
    cuts = (pl.ds(0, first), pl.ds(first, units - first))
    gg_copies = {}
    store_in = pltpu.make_async_copy(wide, in_out, store_sem.at[0])
    for hop in range(far):
        for c in range(2):
            for d in range(2):
                if hop >= near and c != d:
                    continue
                if hop > 0:
                    gg_copies[d, hop - 1, c].wait_recv()
                block = ring_index(place - hop if d == 0 else place + hop, shards)
                view = gg.at[block, cuts[c], :]
                gg_copies[d, hop, c] = remote(
                    view,
                    view,
                    gg_send.at[d, hop, c],
                    gg_recv.at[d, hop, c],
                    (ahead if d == 0 else behind, exp),
                )
        if hop == 0:
            mine = pl.ds(pl.multiple_of(tok * strip_width, 128), strip_width)
            strip[...] = xbuf[:, :, mine].reshape(rows, strip_width).T
            input_tiles(0, tiles // 2)
        if hop == 1:
            input_tiles(tiles // 2, tiles)
            store_in.start()
    for (d, hop, c), copy in gg_copies.items():
        if (d, hop + 1, c) not in gg_copies:
            copy.wait_recv()
    store_gg = pltpu.make_async_copy(gg, gg_out, store_sem.at[1])
    store_gg.start()
    for copy in sent:
        copy.wait_send()
    store_in.wait()
    store_gg.wait()


def local(tokens_x, out_grad, expert_ids, route_q, gate_w, up_w, down_w):
    owners = lax.axis_size("exp")
    shards = lax.axis_size("tok")
    position = lax.axis_index("tok")
    tok_rows = tokens_x.shape[0]
    local_width = tokens_x.shape[1]
    capacity = 2 * tok_rows // owners
    slot_count = capacity * shards
    padded = -(-capacity // 16) * 16
    fitted = expert_ids < owners
    fitted_id = jnp.sum(jnp.where(fitted, expert_ids, 0), axis=1)
    route_weight = jnp.sum(jnp.where(fitted, route_q, 0), axis=1).astype(jnp.float32) / 256.0
    order = jnp.arange(tok_rows, dtype=jnp.int32)
    earlier = (fitted_id[:, None] == fitted_id[None, :]) & (order[:, None] > order[None, :])
    rank_in = jnp.sum(earlier.astype(jnp.int32), axis=1)
    slot_ids = fitted_id * padded + rank_in
    packer = (slot_ids[None, :] == jnp.arange(owners * padded, dtype=jnp.int32)[:, None]).astype(
        jnp.bfloat16
    )
    scaled = (route_weight[:, None] * out_grad.astype(jnp.float32)).astype(jnp.bfloat16)
    packed_x = jnp.dot(packer, tokens_x, preferred_element_type=jnp.float32).astype(jnp.bfloat16)
    packed_x = packed_x.reshape(owners, padded, local_width)
    id_rows = jnp.broadcast_to(slot_ids[None, :], (8, tok_rows))
    full_width = local_width * owners
    units = gate_w.shape[1]
    rows = shards * padded
    far = shards // 2
    vmem = pl.BlockSpec(memory_space=pltpu.VMEM)
    anywhere = pl.BlockSpec(memory_space=pl.ANY)
    dma = pltpu.SemaphoreType.DMA
    input_rows, gg_all = pl.pallas_call(
        functools.partial(exchange_kernel, shards, owners, slot_count),
        out_shape=(
            jax.ShapeDtypeStruct((full_width // shards, full_width), jnp.float32),
            jax.ShapeDtypeStruct((shards, units, rows), jnp.bfloat16),
        ),
        in_specs=[vmem, vmem, vmem, anywhere, anywhere, anywhere],
        out_specs=(anywhere, anywhere),
        scratch_shapes=[
            pltpu.VMEM((shards, padded, full_width), jnp.bfloat16),
            pltpu.VMEM((shards, padded, full_width), jnp.bfloat16),
            pltpu.VMEM((shards, tok_rows, local_width), jnp.bfloat16),
            pltpu.VMEM((shards, owners, padded, local_width), jnp.bfloat16),
            pltpu.VMEM((shards, 8, tok_rows), jnp.int32),
            pltpu.VMEM((units, full_width), jnp.bfloat16),
            pltpu.VMEM((units, full_width), jnp.bfloat16),
            pltpu.VMEM((units, full_width), jnp.bfloat16),
            pltpu.VMEM((units, rows), jnp.float32),
            pltpu.VMEM((units, rows), jnp.float32),
            pltpu.VMEM((shards, units, rows), jnp.bfloat16),
            pltpu.VMEM((full_width // shards, rows), jnp.bfloat16),
            pltpu.VMEM((full_width // shards, full_width), jnp.float32),
            dma((shards,)),
            dma((shards,)),
            dma((shards + 1, owners)),
            dma((shards + 1, owners)),
            dma((shards + 1,)),
            dma((2, 2, far, 2)),
            dma((2, 2, far, 2)),
            dma((2, far, 2)),
            dma((2, far, 2)),
            dma((3,)),
            dma((2,)),
        ],
        compiler_params=pltpu.CompilerParams(
            collective_id=0, has_side_effects=True, vmem_limit_bytes=56 * 2**20
        ),
        cost_estimate=pl.CostEstimate(
            flops=6 * units * rows * full_width,
            bytes_accessed=20 * 2**20,
            transcendentals=units * rows,
        ),
    )(packed_x, scaled, id_rows, gate_w[0], up_w[0], down_w[0])
    grad_cols = lax.dynamic_index_in_dim(gg_all, position, 0, keepdims=False)
    grad_rows = lax.dot_general(
        grad_cols, gg_all.reshape(shards * units, rows), NT, preferred_element_type=jnp.float32
    )
    grad_rows = grad_rows / float(slot_count)
    return (input_rows[None], grad_rows[None])


def solution(mesh):
    placed = (
        P("tok", "exp"),
        P("tok", "exp"),
        P("tok", None),
        P("tok", None),
        P("exp", "tok", None),
        P("exp", "tok", None),
        P("exp", "tok", None),
    )
    return jax.shard_map(
        local,
        mesh=mesh,
        in_specs=placed,
        out_specs=(P("exp", "tok", None), P("exp", "tok", None)),
        check_vma=False,
    )
```

```python
import functools

import jax
import jax.numpy as jnp
from jax import lax
from jax.experimental import pallas as pl
from jax.experimental.pallas import tpu as pltpu
from jax.sharding import PartitionSpec as P

MESH = pl.DeviceIdType.MESH
NT = (((1,), (1,)), ((), ()))


def silu_slope(values):
    sigma = jax.nn.sigmoid(values)
    return sigma * (1.0 + values * (1.0 - sigma))


def ring_place(index, count):
    odd = lax.rem(index, 2)
    half = index // 2
    return (1 - odd) * half + odd * (count - 1 - half)


def ring_index(place, count):
    place = lax.rem(place + 2 * count, count)
    late = place // (count // 2)
    return (1 - late) * (2 * place) + late * (2 * (count - 1 - place) + 1)


def exchange_kernel(
    shards, owners, slot_count,
    x_ref, g_ref, weight_ref, ids_ref, wg_ref, wu_ref, wd_ref,
    in_out, gg_out,
    xbuf, gbuf, raw_own, raw, packed_x, packed, ids, wg, wu, wd, hidden, up, gate, gg, strip, wide,
    ids_send, ids_recv, swap_send, swap_recv, own_sem, ring_send, ring_recv,
    gg_send, gg_recv, load_sem, store_sem,
):
    tok = lax.axis_index("tok")
    exp = lax.axis_index("exp")
    place = ring_place(tok, shards)
    ahead = ring_index(place + 1, shards)
    behind = ring_index(place - 1, shards)
    width = x_ref.shape[1]
    full = xbuf.shape[2]
    cap = xbuf.shape[1]
    rows = shards * cap
    far = shards // 2
    near = (shards - 1) // 2

    barrier = pltpu.get_barrier_semaphore()
    for k in range(1, shards):
        pl.semaphore_signal(
            barrier, inc=1, device_id=(lax.rem(tok + k, shards), exp), device_id_type=MESH
        )
    for k in range(1, owners):
        pl.semaphore_signal(
            barrier, inc=1, device_id=(tok, lax.rem(exp + k, owners)), device_id_type=MESH
        )
    pl.semaphore_wait(barrier, shards + owners - 2)

    sent = []

    def remote(src, dst, send_sem, recv_sem, device):
        copy = pltpu.make_async_remote_copy(
            src_ref=src,
            dst_ref=dst,
            send_sem=send_sem,
            recv_sem=recv_sem,
            device_id=device,
            device_id_type=MESH,
        )
        copy.start()
        sent.append(copy)
        return copy

    copies = {}

    def send(a, d, hop, c):
        block = ring_index(place - hop if d == 0 else place + hop, shards)
        buf = (raw, xbuf)[a]
        half = buf.shape[2] // 2
        view = buf.at[block, :, pl.ds(c * half, half)]
        src = raw_own.at[:, pl.ds(c * half, half)] if a == 0 and hop == 0 else view
        copies[a, d, hop, c] = remote(
            src,
            view,
            ring_send.at[a, d, hop, c],
            ring_recv.at[a, d, hop, c],
            (ahead if d == 0 else behind, exp),
        )

    columns = pl.ds(pl.multiple_of(exp * width, 128), width)
    swaps = []

    def swap(j, source, buf, block):
        for k in range(1, owners):
            peer = lax.rem(exp + k, owners)
            swaps.append((j, remote(
                source(peer),
                buf.at[block, :, columns],
                swap_send.at[j, k],
                swap_recv.at[j, k],
                (tok, peer),
            ).wait_recv))
        own = pltpu.make_async_copy(source(exp), buf.at[block, :, columns], own_sem.at[j])
        own.start()
        swaps.append((j, own.wait))

    slot_iota = lax.broadcasted_iota(jnp.int32, (owners * cap, ids.shape[2]), 0)

    def choose(row, tokens):
        picks = (slot_iota == row).astype(jnp.float32).astype(jnp.bfloat16)
        chosen = jnp.dot(picks, tokens, preferred_element_type=jnp.float32)
        return chosen.astype(jnp.bfloat16).reshape(owners, cap, width)

    def pack(j, block, row, tokens):
        packed[block] = choose(row, tokens)
        swap(j, lambda e: packed.at[block, e], gbuf, block)

    id_copies = []

    orders = (
        [(0, h) for h in range(far)] + [(1, h) for h in range(near)],
        [(0, h) for h in range(near)] + [(1, h) for h in range(far)],
    )
    raw_own[...] = (weight_ref[...] * g_ref[...].astype(jnp.float32)).astype(raw.dtype)
    for c in range(2):
        for d in range(2):
            send(0, d, 0, c)
    for k in range(1, shards):
        id_copies.append(remote(
            ids_ref, ids.at[tok], ids_send.at[k], ids_recv.at[k], (lax.rem(tok + k, shards), exp)
        ))
    packed_x[...] = choose(ids_ref[0:1, :], x_ref[...])
    swap(0, lambda e: packed_x.at[e], xbuf, tok)
    pack(1, tok, ids_ref[0:1, :], raw_own[...])
    number = 2

    loads = []
    for i, (src, dst) in enumerate(((wd_ref, wd), (wg_ref, wg), (wu_ref, wu))):
        load = pltpu.make_async_copy(src, dst, load_sem.at[i])
        load.start()
        loads.append(load)

    for copy in id_copies:
        copy.wait_recv()

    x_ready = False
    for s in range(1, far + near):
        landed = []
        for c in range(2):
            for d in range(2):
                a, hop = orders[d][s - 1]
                copies[a, d, hop, c].wait_recv()
                if c == 1 and a == 0:
                    landed.append((d, hop + 1))
                if orders[d][s] == (1, 0) and not x_ready:
                    for j, wait in swaps:
                        if j == 0:
                            wait()
                    x_ready = True
                send(*(orders[d][s][0], d, orders[d][s][1], c))
        for d, hop in landed:
            block = ring_index(place - hop if d == 0 else place + hop, shards)
            pack(number, block, ids[block, 0:1, :], raw[block])
            number += 1

    step = min(1024, full)
    parts = full // step

    def product(weights, buf, acc, low, high):
        def body(i, carry):
            part = pl.ds(pl.multiple_of(i * step, step), step)
            acc[...] += lax.dot_general(
                weights[:, part],
                buf[:, :, part].reshape(rows, step),
                NT,
                preferred_element_type=jnp.float32,
            )
            return carry

        lax.fori_loop(low, high, body, 0)

    for acc in (hidden, up, gate):
        acc[...] = jnp.zeros_like(acc)
    for j, wait in swaps:
        if j > 0:
            wait()
    for load in loads:
        load.wait()
    product(wd, gbuf, hidden, 0, parts)
    for c in range(2):
        for d in range(2):
            copies[1, d, orders[d][-1][1], c].wait_recv()
        for weights, acc in ((wu, up), (wg, gate)):
            product(weights, xbuf, acc, c * parts // 2, (c + 1) * parts // 2)
    gg[tok] = (hidden[...] * up[...] * silu_slope(gate[...])).astype(gg.dtype)

    tile = min(512, full)
    tiles = full // tile
    strip_width = strip.shape[0]

    def input_tiles(low, high):
        def body(i, carry):
            part = pl.ds(pl.multiple_of(i * tile, tile), tile)
            total = jnp.dot(
                strip[...], xbuf[:, :, part].reshape(rows, tile), preferred_element_type=jnp.float32
            )
            wide[:, part] = total / float(slot_count)
            return carry

        lax.fori_loop(low, high, body, 0)

    units = gg.shape[1]
    first = -(-(units // 2) // 16) * 16
    cuts = (pl.ds(0, first), pl.ds(first, units - first))
    gg_copies = {}
    store_in = pltpu.make_async_copy(wide, in_out, store_sem.at[0])
    for hop in range(far):
        for c in range(2):
            for d in range(2):
                if hop >= near and c != d:
                    continue
                if hop > 0:
                    gg_copies[d, hop - 1, c].wait_recv()
                block = ring_index(place - hop if d == 0 else place + hop, shards)
                view = gg.at[block, cuts[c], :]
                gg_copies[d, hop, c] = remote(
                    view,
                    view,
                    gg_send.at[d, hop, c],
                    gg_recv.at[d, hop, c],
                    (ahead if d == 0 else behind, exp),
                )
        if hop == 0:
            mine = pl.ds(pl.multiple_of(tok * strip_width, 128), strip_width)
            strip[...] = xbuf[:, :, mine].reshape(rows, strip_width).T
            input_tiles(0, tiles // 2)
        if hop == 1:
            input_tiles(tiles // 2, tiles)
            store_in.start()
    for (d, hop, c), copy in gg_copies.items():
        if (d, hop + 1, c) not in gg_copies:
            copy.wait_recv()
    store_gg = pltpu.make_async_copy(gg, gg_out, store_sem.at[1])
    store_gg.start()
    for copy in sent:
        copy.wait_send()
    store_in.wait()
    store_gg.wait()


def finish_kernel(slot_count, wide_ref, gg_ref, in_out, grad_out, sems):
    strips = sems.shape[0]
    rows = wide_ref.shape[0] // strips
    copies = []
    for i in range(strips):
        part = pl.ds(i * rows, rows)
        copy = pltpu.make_async_copy(wide_ref.at[part, :], in_out.at[part, :], sems.at[i])
        copy.start()
        copies.append(copy)
    shards, units, slots = gg_ref.shape
    total = lax.dot_general(
        gg_ref[lax.axis_index("tok")],
        gg_ref[...].reshape(shards * units, slots),
        NT,
        preferred_element_type=jnp.float32,
    )
    grad_out[...] = total / float(slot_count)
    for copy in copies:
        copy.wait()


def local(tokens_x, out_grad, expert_ids, route_q, gate_w, up_w, down_w):
    owners = lax.axis_size("exp")
    shards = lax.axis_size("tok")
    position = lax.axis_index("tok")
    tok_rows = tokens_x.shape[0]
    local_width = tokens_x.shape[1]
    capacity = 2 * tok_rows // owners
    slot_count = capacity * shards
    padded = -(-capacity // 16) * 16
    fitted = expert_ids < owners
    fitted_id = jnp.sum(jnp.where(fitted, expert_ids, 0), axis=1)
    route_weight = jnp.sum(jnp.where(fitted, route_q, 0), axis=1).astype(jnp.float32) / 256.0
    order = jnp.arange(tok_rows, dtype=jnp.int32)
    earlier = (fitted_id[:, None] == fitted_id[None, :]) & (order[:, None] > order[None, :])
    rank_in = jnp.sum(earlier.astype(jnp.int32), axis=1)
    slot_ids = fitted_id * padded + rank_in
    id_rows = jnp.broadcast_to(slot_ids[None, :], (8, tok_rows))
    full_width = local_width * owners
    units = gate_w.shape[1]
    rows = shards * padded
    far = shards // 2
    vmem = pl.BlockSpec(memory_space=pltpu.VMEM)
    anywhere = pl.BlockSpec(memory_space=pl.ANY)
    dma = pltpu.SemaphoreType.DMA
    wide, gg_all = pl.pallas_call(
        functools.partial(exchange_kernel, shards, owners, slot_count),
        out_shape=(
            jax.ShapeDtypeStruct((full_width // shards, full_width), jnp.float32),
            jax.ShapeDtypeStruct((shards, units, rows), jnp.bfloat16),
        ),
        in_specs=[vmem, vmem, vmem, vmem, anywhere, anywhere, anywhere],
        out_specs=(anywhere, anywhere),
        scratch_shapes=[
            pltpu.VMEM((shards, padded, full_width), jnp.bfloat16),
            pltpu.VMEM((shards, padded, full_width), jnp.bfloat16),
            pltpu.VMEM((tok_rows, local_width), jnp.bfloat16),
            pltpu.VMEM((shards, tok_rows, local_width), jnp.bfloat16),
            pltpu.VMEM((owners, padded, local_width), jnp.bfloat16),
            pltpu.VMEM((shards, owners, padded, local_width), jnp.bfloat16),
            pltpu.VMEM((shards, 8, tok_rows), jnp.int32),
            pltpu.VMEM((units, full_width), jnp.bfloat16),
            pltpu.VMEM((units, full_width), jnp.bfloat16),
            pltpu.VMEM((units, full_width), jnp.bfloat16),
            pltpu.VMEM((units, rows), jnp.float32),
            pltpu.VMEM((units, rows), jnp.float32),
            pltpu.VMEM((units, rows), jnp.float32),
            pltpu.VMEM((shards, units, rows), jnp.bfloat16),
            pltpu.VMEM((full_width // shards, rows), jnp.bfloat16),
            pltpu.VMEM((full_width // shards, full_width), jnp.float32),
            dma((shards,)),
            dma((shards,)),
            dma((shards + 1, owners)),
            dma((shards + 1, owners)),
            dma((shards + 1,)),
            dma((2, 2, far, 2)),
            dma((2, 2, far, 2)),
            dma((2, far, 2)),
            dma((2, far, 2)),
            dma((3,)),
            dma((2,)),
        ],
        compiler_params=pltpu.CompilerParams(
            collective_id=0, has_side_effects=True, vmem_limit_bytes=56 * 2**20
        ),
        cost_estimate=pl.CostEstimate(
            flops=6 * units * rows * full_width,
            bytes_accessed=20 * 2**20,
            transcendentals=units * rows,
        ),
    )(tokens_x, out_grad, route_weight[:, None], id_rows, gate_w[0], up_w[0], down_w[0])
    input_rows, grad_rows = pl.pallas_call(
        functools.partial(finish_kernel, slot_count),
        out_shape=(
            jax.ShapeDtypeStruct((full_width // shards, full_width), jnp.float32),
            jax.ShapeDtypeStruct((units, shards * units), jnp.float32),
        ),
        in_specs=[anywhere, vmem],
        out_specs=(anywhere, vmem),
        scratch_shapes=[dma((8,))],
        compiler_params=pltpu.CompilerParams(vmem_limit_bytes=56 * 2**20),
    )(wide, gg_all)
    return (input_rows[None], grad_rows[None])


def solution(mesh):
    placed = (
        P("tok", "exp"),
        P("tok", "exp"),
        P("tok", None),
        P("tok", None),
        P("exp", "tok", None),
        P("exp", "tok", None),
        P("exp", "tok", None),
    )
    return jax.shard_map(
        local,
        mesh=mesh,
        in_specs=placed,
        out_specs=(P("exp", "tok", None), P("exp", "tok", None)),
        check_vma=False,
    )
```

```python
import functools

import jax
import jax.numpy as jnp
from jax import lax
from jax.experimental import pallas as pl
from jax.experimental.pallas import tpu as pltpu
from jax.sharding import PartitionSpec as P

MESH = pl.DeviceIdType.MESH
NT = (((1,), (1,)), ((), ()))


def silu_slope(values):
    sigma = jax.nn.sigmoid(values)
    return sigma * (1.0 + values * (1.0 - sigma))


def ring_place(index, count):
    odd = lax.rem(index, 2)
    half = index // 2
    return (1 - odd) * half + odd * (count - 1 - half)


def ring_index(place, count):
    place = lax.rem(place + 2 * count, count)
    late = place // (count // 2)
    return (1 - late) * (2 * place) + late * (2 * (count - 1 - place) + 1)


def exchange_kernel(
    shards, owners, slot_count,
    x_ref, g_ref, weight_ref, ids_ref, wg_ref, wu_ref, wd_ref,
    in_out, gg_out,
    xbuf, gbuf, raw_own, raw, packed_x, packed, ids, wg, wu, wd, hidden, up, gate, gg, strip, wide,
    ids_send, ids_recv, swap_send, swap_recv, own_sem, ring_send, ring_recv,
    gg_send, gg_recv, load_sem, store_sem,
):
    tok = lax.axis_index("tok")
    exp = lax.axis_index("exp")
    place = ring_place(tok, shards)
    ahead = ring_index(place + 1, shards)
    behind = ring_index(place - 1, shards)
    width = x_ref.shape[1]
    full = xbuf.shape[2]
    cap = xbuf.shape[1]
    rows = shards * cap
    far = shards // 2
    near = (shards - 1) // 2

    barrier = pltpu.get_barrier_semaphore()
    for k in range(1, shards):
        pl.semaphore_signal(
            barrier, inc=1, device_id=(lax.rem(tok + k, shards), exp), device_id_type=MESH
        )
    for k in range(1, owners):
        pl.semaphore_signal(
            barrier, inc=1, device_id=(tok, lax.rem(exp + k, owners)), device_id_type=MESH
        )
    pl.semaphore_wait(barrier, shards + owners - 2)

    sent = []

    def remote(src, dst, send_sem, recv_sem, device):
        copy = pltpu.make_async_remote_copy(
            src_ref=src,
            dst_ref=dst,
            send_sem=send_sem,
            recv_sem=recv_sem,
            device_id=device,
            device_id_type=MESH,
        )
        copy.start()
        sent.append(copy)
        return copy

    copies = {}

    def send(a, d, hop, c):
        block = ring_index(place - hop if d == 0 else place + hop, shards)
        buf = (raw, xbuf)[a]
        half = buf.shape[2] // 2
        view = buf.at[block, :, pl.ds(c * half, half)]
        src = raw_own.at[:, pl.ds(c * half, half)] if a == 0 and hop == 0 else view
        copies[a, d, hop, c] = remote(
            src,
            view,
            ring_send.at[a, d, hop, c],
            ring_recv.at[a, d, hop, c],
            (ahead if d == 0 else behind, exp),
        )

    columns = pl.ds(pl.multiple_of(exp * width, 128), width)
    swaps = []

    def swap(j, source, buf, block):
        for k in range(1, owners):
            peer = lax.rem(exp + k, owners)
            swaps.append((j, remote(
                source(peer),
                buf.at[block, :, columns],
                swap_send.at[j, k],
                swap_recv.at[j, k],
                (tok, peer),
            ).wait_recv))
        own = pltpu.make_async_copy(source(exp), buf.at[block, :, columns], own_sem.at[j])
        own.start()
        swaps.append((j, own.wait))

    slot_iota = lax.broadcasted_iota(jnp.int32, (owners * cap, ids.shape[2]), 0)

    def choose(row, tokens):
        picks = (slot_iota == row).astype(jnp.float32).astype(jnp.bfloat16)
        chosen = jnp.dot(picks, tokens, preferred_element_type=jnp.float32)
        return chosen.astype(jnp.bfloat16).reshape(owners, cap, width)

    def pack(j, block, row, tokens):
        packed[block] = choose(row, tokens)
        swap(j, lambda e: packed.at[block, e], gbuf, block)

    id_copies = []

    orders = (
        [(0, h) for h in range(far)] + [(1, h) for h in range(near)],
        [(0, h) for h in range(near)] + [(1, h) for h in range(far)],
    )
    raw_own[...] = (weight_ref[...] * g_ref[...].astype(jnp.float32)).astype(raw.dtype)
    for c in range(2):
        for d in range(2):
            send(0, d, 0, c)
    for k in range(1, shards):
        id_copies.append(remote(
            ids_ref, ids.at[tok], ids_send.at[k], ids_recv.at[k], (lax.rem(tok + k, shards), exp)
        ))
    packed_x[...] = choose(ids_ref[0:1, :], x_ref[...])
    swap(0, lambda e: packed_x.at[e], xbuf, tok)
    pack(1, tok, ids_ref[0:1, :], raw_own[...])
    number = 2

    loads = []
    for i, (src, dst) in enumerate(((wd_ref, wd), (wg_ref, wg), (wu_ref, wu))):
        load = pltpu.make_async_copy(src, dst, load_sem.at[i])
        load.start()
        loads.append(load)

    for copy in id_copies:
        copy.wait_recv()

    x_ready = False
    for s in range(1, far + near):
        landed = []
        for c in range(2):
            for d in range(2):
                a, hop = orders[d][s - 1]
                copies[a, d, hop, c].wait_recv()
                if c == 1 and a == 0:
                    landed.append((d, hop + 1))
                if orders[d][s] == (1, 0) and not x_ready:
                    for j, wait in swaps:
                        if j == 0:
                            wait()
                    x_ready = True
                send(*(orders[d][s][0], d, orders[d][s][1], c))
        for d, hop in landed:
            block = ring_index(place - hop if d == 0 else place + hop, shards)
            pack(number, block, ids[block, 0:1, :], raw[block])
            number += 1

    step = min(1024, full)
    parts = full // step

    def product(weights, buf, acc, low, high):
        def body(i, carry):
            part = pl.ds(pl.multiple_of(i * step, step), step)
            acc[...] += lax.dot_general(
                weights[:, part],
                buf[:, :, part].reshape(rows, step),
                NT,
                preferred_element_type=jnp.float32,
            )
            return carry

        lax.fori_loop(low, high, body, 0)

    for acc in (hidden, up, gate):
        acc[...] = jnp.zeros_like(acc)
    for j, wait in swaps:
        if j > 0:
            wait()
    for load in loads:
        load.wait()
    product(wd, gbuf, hidden, 0, parts)
    for c in range(2):
        for d in range(2):
            copies[1, d, orders[d][-1][1], c].wait_recv()
        for weights, acc in ((wu, up), (wg, gate)):
            product(weights, xbuf, acc, c * parts // 2, (c + 1) * parts // 2)
    gg[tok] = (hidden[...] * up[...] * silu_slope(gate[...])).astype(gg.dtype)

    tile = min(512, full)
    tiles = full // tile
    strip_width = strip.shape[0]

    def input_tiles(low, high):
        def body(i, carry):
            part = pl.ds(pl.multiple_of(i * tile, tile), tile)
            total = jnp.dot(
                strip[...], xbuf[:, :, part].reshape(rows, tile), preferred_element_type=jnp.float32
            )
            wide[:, part] = total / float(slot_count)
            return carry

        lax.fori_loop(low, high, body, 0)

    units = gg.shape[1]
    first = -(-(units // 2) // 16) * 16
    cuts = (pl.ds(0, first), pl.ds(first, units - first))
    gg_copies = {}
    store_in = pltpu.make_async_copy(wide, in_out, store_sem.at[0])
    for hop in range(far):
        for c in range(2):
            for d in range(2):
                if hop >= near and c != d:
                    continue
                if hop > 0:
                    gg_copies[d, hop - 1, c].wait_recv()
                block = ring_index(place - hop if d == 0 else place + hop, shards)
                view = gg.at[block, cuts[c], :]
                gg_copies[d, hop, c] = remote(
                    view,
                    view,
                    gg_send.at[d, hop, c],
                    gg_recv.at[d, hop, c],
                    (ahead if d == 0 else behind, exp),
                )
        if hop == 0:
            mine = pl.ds(pl.multiple_of(tok * strip_width, 128), strip_width)
            strip[...] = xbuf[:, :, mine].reshape(rows, strip_width).T
            input_tiles(0, tiles // 2)
        if hop == 1:
            input_tiles(tiles // 2, tiles)
            store_in.start()
    for (d, hop, c), copy in gg_copies.items():
        if (d, hop + 1, c) not in gg_copies:
            copy.wait_recv()
    store_gg = pltpu.make_async_copy(gg, gg_out, store_sem.at[1])
    store_gg.start()
    for copy in sent:
        copy.wait_send()
    store_in.wait()
    store_gg.wait()


def finish_kernel(slot_count, wide_ref, gg_ref, in_out, grad_out, held, load_sems, store_sems):
    strips = load_sems.shape[0]
    rows = wide_ref.shape[0] // strips
    loads, stores = [], []
    for i in range(strips):
        part = pl.ds(i * rows, rows)
        load = pltpu.make_async_copy(wide_ref.at[part, :], held.at[part, :], load_sems.at[i])
        load.start()
        loads.append(load)
        stores.append(pltpu.make_async_copy(held.at[part, :], in_out.at[part, :], store_sems.at[i]))
    for load, store in zip(loads, stores):
        load.wait()
        store.start()
    shards, units, slots = gg_ref.shape
    total = lax.dot_general(
        gg_ref[lax.axis_index("tok")],
        gg_ref[...].reshape(shards * units, slots),
        NT,
        preferred_element_type=jnp.float32,
    )
    grad_out[...] = total / float(slot_count)
    for store in stores:
        store.wait()


def local(tokens_x, out_grad, expert_ids, route_q, gate_w, up_w, down_w):
    owners = lax.axis_size("exp")
    shards = lax.axis_size("tok")
    position = lax.axis_index("tok")
    tok_rows = tokens_x.shape[0]
    local_width = tokens_x.shape[1]
    capacity = 2 * tok_rows // owners
    slot_count = capacity * shards
    padded = -(-capacity // 16) * 16
    fitted = expert_ids < owners
    fitted_id = jnp.sum(jnp.where(fitted, expert_ids, 0), axis=1)
    route_weight = jnp.sum(jnp.where(fitted, route_q, 0), axis=1).astype(jnp.float32) / 256.0
    order = jnp.arange(tok_rows, dtype=jnp.int32)
    earlier = (fitted_id[:, None] == fitted_id[None, :]) & (order[:, None] > order[None, :])
    rank_in = jnp.sum(earlier.astype(jnp.int32), axis=1)
    slot_ids = fitted_id * padded + rank_in
    id_rows = jnp.broadcast_to(slot_ids[None, :], (8, tok_rows))
    full_width = local_width * owners
    units = gate_w.shape[1]
    rows = shards * padded
    far = shards // 2
    vmem = pl.BlockSpec(memory_space=pltpu.VMEM)
    anywhere = pl.BlockSpec(memory_space=pl.ANY)
    dma = pltpu.SemaphoreType.DMA
    wide, gg_all = pl.pallas_call(
        functools.partial(exchange_kernel, shards, owners, slot_count),
        out_shape=(
            jax.ShapeDtypeStruct((full_width // shards, full_width), jnp.float32),
            jax.ShapeDtypeStruct((shards, units, rows), jnp.bfloat16),
        ),
        in_specs=[vmem, vmem, vmem, vmem, anywhere, anywhere, anywhere],
        out_specs=(anywhere, anywhere),
        scratch_shapes=[
            pltpu.VMEM((shards, padded, full_width), jnp.bfloat16),
            pltpu.VMEM((shards, padded, full_width), jnp.bfloat16),
            pltpu.VMEM((tok_rows, local_width), jnp.bfloat16),
            pltpu.VMEM((shards, tok_rows, local_width), jnp.bfloat16),
            pltpu.VMEM((owners, padded, local_width), jnp.bfloat16),
            pltpu.VMEM((shards, owners, padded, local_width), jnp.bfloat16),
            pltpu.VMEM((shards, 8, tok_rows), jnp.int32),
            pltpu.VMEM((units, full_width), jnp.bfloat16),
            pltpu.VMEM((units, full_width), jnp.bfloat16),
            pltpu.VMEM((units, full_width), jnp.bfloat16),
            pltpu.VMEM((units, rows), jnp.float32),
            pltpu.VMEM((units, rows), jnp.float32),
            pltpu.VMEM((units, rows), jnp.float32),
            pltpu.VMEM((shards, units, rows), jnp.bfloat16),
            pltpu.VMEM((full_width // shards, rows), jnp.bfloat16),
            pltpu.VMEM((full_width // shards, full_width), jnp.float32),
            dma((shards,)),
            dma((shards,)),
            dma((shards + 1, owners)),
            dma((shards + 1, owners)),
            dma((shards + 1,)),
            dma((2, 2, far, 2)),
            dma((2, 2, far, 2)),
            dma((2, far, 2)),
            dma((2, far, 2)),
            dma((3,)),
            dma((2,)),
        ],
        compiler_params=pltpu.CompilerParams(
            collective_id=0, has_side_effects=True, vmem_limit_bytes=56 * 2**20
        ),
        cost_estimate=pl.CostEstimate(
            flops=6 * units * rows * full_width,
            bytes_accessed=20 * 2**20,
            transcendentals=units * rows,
        ),
    )(tokens_x, out_grad, route_weight[:, None], id_rows, gate_w[0], up_w[0], down_w[0])
    input_rows, grad_rows = pl.pallas_call(
        functools.partial(finish_kernel, slot_count),
        out_shape=(
            jax.ShapeDtypeStruct((full_width // shards, full_width), jnp.float32),
            jax.ShapeDtypeStruct((units, shards * units), jnp.float32),
        ),
        in_specs=[anywhere, vmem],
        out_specs=(anywhere, vmem),
        scratch_shapes=[
            pltpu.VMEM((full_width // shards, full_width), jnp.float32),
            dma((8,)),
            dma((8,)),
        ],
        compiler_params=pltpu.CompilerParams(vmem_limit_bytes=56 * 2**20),
    )(wide, gg_all)
    return (input_rows[None], grad_rows[None])


def solution(mesh):
    placed = (
        P("tok", "exp"),
        P("tok", "exp"),
        P("tok", None),
        P("tok", None),
        P("exp", "tok", None),
        P("exp", "tok", None),
        P("exp", "tok", None),
    )
    return jax.shard_map(
        local,
        mesh=mesh,
        in_specs=placed,
        out_specs=(P("exp", "tok", None), P("exp", "tok", None)),
        check_vma=False,
    )
```
